32 devices in a mesh: groups: 2 (over y), expert: 8 (over z, x), tensor: 2 (over core).
Axes of the slice: x: 2, y: 2, z: 4, core: 2. Of those that a mesh axis runs over, the one named last changes fastest.
Arguments:
- residual: bfloat16 [2, 384, 2880], P(None, ('groups', 'expert'), 'tensor'), parts along dimension 1, may hold values from -16 to 16
- queries: bfloat16 [2, 384, 2048], P(None, ('groups', 'expert'), 'tensor'), parts along dimension 1, may hold values from -24 to 24
- new_kv: bfloat16 [2, 384, 2, 512], P(None, ('groups', 'expert'), None, 'tensor'), parts along dimension 1, may hold values from -6 to 6
- kv_cache: bfloat16 [384, 2, 8, 32, 64], P(('groups', 'expert'), None, 'tensor'), parts along dimension 0, may hold values from -6 to 6
- lengths: int32 [384], P(('groups', 'expert')), parts along dimension 0, may hold values from 2 to 32, as said below
- sink_logits: float32 [32], P('tensor'), may hold values from -5 to 5
- out_proj: bfloat16 [2048, 2880], P('tensor'), may hold values from -0.125 to 0.125
- norm_gain: bfloat16 [2880], replicated, may hold values from 0.25 to 1.75
- expert_ids: int32 [2, 384, 4], P(None, ('groups', 'expert')), parts along dimension 1, may hold values from 0 to 7, all different within a row; in each aligned block of 24 rows (0 to 23, 24 to 47, ..., all dimensions but the last counted through in order) at most 24 rows name the same one
- gate_weights: float32 [2, 384, 4], P(None, ('groups', 'expert')), parts along dimension 1, may hold values from 0.1 to 1
- w_gate_up: bfloat16 [8, 2880, 2, 1536], P('expert', None, None, 'tensor'), may hold values from -0.109375 to 0.109375
- w_down: bfloat16 [8, 1536, 2880], P('expert', 'tensor'), may hold values from -0.15625 to 0.15625
Outputs:
- layer_out: bfloat16 [2, 384, 2880], P(None, ('groups', 'expert'), 'tensor'), parts along dimension 1
The draws below stay inside these ranges and needn't reach their ends.
There are 2 independent parts, one for each index of `groups`. The reference program is written for one: setup_inputs(seed, part) draws one part's arguments, and reference() takes and returns one part's arrays. A program takes and returns all parts, laid end to end along the dimension named above; an argument that names none is the same for every part. Nothing has to cross between parts.
Inputs may be any that keep to these rules, and one draw needn't show every extreme that they name: `expert_ids`: among the rows that one device holds in one step, no expert is named more than 24 times, a bound that some block reaches. `lengths`: on every device some row uses all 32 cache positions.
All inputs are finite; a program needn't handle non-finite values.
Results may differ from the reference program's by a relative error of at most 0.0075.
Values may be sent and summed in bfloat16 or wider, within the bound.
A program may use at most 128 MiB of HBM per device.

```python
import math
import jax
import jax.numpy as jnp
import numpy as np
from jax import lax

D = 2880
FF = 1536
QH = 32
KVH = 8
HD = 64
TOP = 4
STEPS = 2
CACHE = 32
ROWS_DEV = 24
EXPERTS = 8
ROWS = 192
CAP = 24
N_EXPERT = 8
N_TENSOR = 2


def draw_queries(key, part):
    key = jax.random.fold_in(key, 21)
    values = jnp.clip(jax.random.normal(key, (STEPS, ROWS, QH * HD), jnp.float32), -6.0, 6.0)
    return values.astype(jnp.bfloat16)


def draw_kv_cache(key, part):
    key = jax.random.fold_in(key, 22)
    values = jnp.clip(jax.random.normal(key, (ROWS, 2, KVH, CACHE, HD), jnp.float32), -6.0, 6.0)
    return values.astype(jnp.bfloat16)


def draw_residual(key, part):
    key = jax.random.fold_in(key, 23)
    values = jnp.clip(jax.random.normal(key, (STEPS, ROWS, D), jnp.float32), -6.0, 6.0)
    return values.astype(jnp.bfloat16)


def draw_lengths(key, part):
    key = jax.random.fold_in(key, 24)
    length_key = jax.random.fold_in(key, 1)
    chosen_key = jax.random.fold_in(key, 2)
    drawn = jax.random.randint(length_key, (ROWS,), 2, CACHE + 1)
    chosen = jax.random.randint(chosen_key, (ROWS // ROWS_DEV,), 0, ROWS_DEV)
    row_index = jnp.arange(ROWS, dtype=jnp.int32)
    longest = row_index % ROWS_DEV == chosen[row_index // ROWS_DEV]
    return jnp.where(longest, CACHE, drawn).astype(jnp.int32)


def block_scale(rng, shape, cuts, smallest, largest):
    level, own = 1.0, jax.random.fold_in(rng, 6)
    for position, parts in cuts:
        draws = jnp.exp(jax.random.uniform(jax.random.fold_in(own, position), (parts,), jnp.float32, smallest / len(cuts), largest / len(cuts)))
        level = level * jnp.repeat(draws, shape[position] // parts).reshape([-1 if axis == position else 1 for axis in range(len(shape))])
    return level


def routed_block(key, own, number, rows, count, top, limit, lean):
    ranking = jax.random.permutation(key, count)
    crowded, common = portions_of(count, rows * top, limit, lean, True), portions_of(count, rows * top, limit, lean, False)
    places = jnp.arange(count)

    def named(sizes, turn):
        used = int((sizes > 0).sum())
        fixed = max(1, used // 4)
        passed = fixed + (places - fixed + turn * (used - fixed)) % max(1, count - fixed)
        return jnp.zeros((count,), jnp.int32).at[ranking[jnp.where(places < fixed, places, passed)]].set(jnp.asarray(sizes, jnp.int32))

    sizes = jnp.where(number % 4 == 0, named(crowded, number // 4), named(common, number - number // 4 - 1))
    mixed = jax.random.permutation(jax.random.fold_in(own, 3), count)
    donor, taker = mixed[0:count // 2 * 2:2], mixed[1:count // 2 * 2:2]
    margin = jnp.minimum(sizes[donor] - 1, limit - sizes[taker]) // 2
    margin = jnp.where((donor == ranking[0]) | (taker == ranking[0]) | (sizes[taker] == 0), 0, jnp.maximum(margin, 0))
    passed = jax.random.randint(jax.random.fold_in(own, 4), (count // 2,), 0, 1 << 20) % (margin + 1)
    sizes = sizes.at[donor].add(-passed).at[taker].add(passed)
    items = jnp.searchsorted(jnp.cumsum(sizes), jnp.arange(rows * top), side="right").astype(jnp.int32)
    grid = items.reshape(top, rows).T
    grid = grid[jax.random.permutation(jax.random.fold_in(own, 1), rows)]
    turn = jax.random.randint(jax.random.fold_in(own, 2), (rows, 1), 0, top)
    return jnp.take_along_axis(grid, (jnp.arange(top)[None, :] + turn) % top, axis=1)


def portions_of(count, total, bound, slope, full):
    portions = [(1 << 20) // math.isqrt(standing ** slope) + 1 for standing in range(1, count + 1)]
    largest = bound if full else min(bound, max(-(-total // count), total * portions[0] // sum(portions)))
    least = 1 if total - largest >= count - 1 else 0
    counts, rest = [largest] + [least] * (count - 1), total - largest - least * (count - 1)
    while rest > 0:
        movable = [i for i in range(1, count) if counts[i] < largest] or [i for i in range(1, count) if counts[i] < bound]
        pool, left = sum([portions[i] for i in movable]), rest
        for i in movable:
            addition = min(bound - counts[i], max(1, left * portions[i] // pool), rest)
            counts[i] = counts[i] + addition
            rest = rest - addition
    return np.array(counts)


def noise(rng, shape, deviation, bound, split=(), held_as=jnp.bfloat16):
    values = deviation * jax.random.normal(rng, shape, jnp.float32)
    if split:
        values = values * block_scale(rng, shape, split, -0.22, 0.18)
    return jnp.clip(values, -bound, bound).astype(held_as)


def setup_inputs(seed: int = 0, part: int = 0) -> dict:
    key_list = jax.random.split(jax.random.key(seed), 13)
    part_keys = jax.random.split(jax.random.fold_in(key_list[12], part), 13)
    residual = draw_residual(jax.random.fold_in(jax.random.fold_in(key_list[12], part), 71), part)
    queries = draw_queries(jax.random.fold_in(jax.random.fold_in(key_list[12], part), 71), part)
    new_kv = noise(part_keys[2], (STEPS, ROWS, 2, KVH * HD), 1.0, 6.0, ((1, 8), (3, 2)))
    kv_cache = draw_kv_cache(jax.random.fold_in(jax.random.fold_in(key_list[12], part), 71), part)
    lengths = draw_lengths(jax.random.fold_in(jax.random.fold_in(key_list[12], part), 71), part)
    sink_logits = noise(key_list[5], (QH,), 1.5, 5.0, ((0, 2),), jnp.float32)
    out_proj = noise(key_list[6], (QH * HD, D), (QH * HD) ** -0.5, 0.125, ((0, 2),))
    norm_gain = jnp.clip(1.0 + 0.15 * jax.random.normal(key_list[7], (D,), jnp.float32), 0.25, 1.75).astype(jnp.bfloat16)
    expert_ids_keys = jax.random.split(jax.random.fold_in(part_keys[8], 1), STEPS * ROWS // ROWS_DEV)
    expert_ids_turns = jax.random.permutation(jax.random.fold_in(part_keys[8], 3), STEPS * ROWS // ROWS_DEV)
    expert_ids = jax.vmap(lambda own, number: routed_block(jax.random.fold_in(part_keys[8], 2), own, number, ROWS_DEV, EXPERTS, TOP, CAP, 2))(expert_ids_keys, expert_ids_turns).reshape((STEPS, ROWS, TOP))
    gate_weights = jnp.clip(jnp.exp(math.log(1.0) - 2.3025851 * jax.random.uniform(part_keys[9], (STEPS, ROWS, TOP), jnp.float32) ** block_scale(part_keys[9], (STEPS, ROWS, TOP), ((1, 8),), -0.2, 0.2)), 0.1, 1.0)
    w_gate_up = noise(key_list[10], (EXPERTS, D, 2, FF), D ** -0.5, 0.109375, ((0, 8), (3, 2)))
    w_down = noise(key_list[11], (EXPERTS, FF, D), FF ** -0.5, 0.15625, ((0, 8), (1, 2)))
    return {"residual": residual, "queries": queries, "new_kv": new_kv, "kv_cache": kv_cache, "lengths": lengths, "sink_logits": sink_logits, "out_proj": out_proj, "norm_gain": norm_gain, "expert_ids": expert_ids, "gate_weights": gate_weights, "w_gate_up": w_gate_up, "w_down": w_down}


def attend(queries_now, key_all, value_all, valid, sink_logits):
    scores = jnp.einsum('rkgd,rkjd->rkgj', queries_now.astype(jnp.float32), key_all.astype(jnp.float32)) * HD ** (-0.5)
    scores = jnp.where(valid[:, None, None, :], scores, -jnp.inf)
    sinks = sink_logits.reshape(1, queries_now.shape[1], queries_now.shape[2], 1)
    peak = jnp.maximum(lax.optimization_barrier(jnp.max(scores, axis=3, keepdims=True)), sinks)
    weights = jnp.where(valid[:, None, None, :], jnp.exp(scores - peak), 0.0)
    totals = lax.optimization_barrier(jnp.sum(weights, axis=3, keepdims=True)) + jnp.exp(sinks - peak)
    probs = (weights / totals).astype(jnp.bfloat16)
    mixed = jnp.einsum('rkgj,rkjd->rkgd', probs.astype(jnp.float32), value_all.astype(jnp.float32))
    return mixed.astype(jnp.bfloat16).reshape(queries_now.shape[0], -1)

def mixture_of_experts(normed, expert_now, weight_now, w_gate_up, w_down):
    pair_count = ROWS * TOP
    most = N_EXPERT * CAP
    hidden_local = FF // N_TENSOR
    flat_ids = expert_now.reshape(-1)
    flat_weights = weight_now.reshape(-1)
    pair_index = jnp.arange(pair_count, dtype=jnp.int32)

    def one_expert(accumulated, expert):
        chosen = flat_ids == expert
        order = jnp.cumsum(chosen.astype(jnp.int32)) - 1
        target = jnp.where(chosen, order, most).astype(jnp.int32)
        members = jnp.zeros((most,), jnp.int32).at[target].set(pair_index, mode='drop')
        member_weight = jnp.zeros((most,), jnp.float32).at[target].set(flat_weights, mode='drop')
        member_rows = members // TOP
        inputs = normed[member_rows]
        w_in = lax.dynamic_index_in_dim(w_gate_up, expert, 0, keepdims=False).reshape(D, 2 * FF)
        w_out = lax.dynamic_index_in_dim(w_down, expert, 0, keepdims=False)
        gate_up = jnp.dot(inputs, w_in, preferred_element_type=jnp.float32).reshape(most, 2, FF)
        gate_part = gate_up[:, 0, :]
        up_part = gate_up[:, 1, :]
        activation = (gate_part * jax.nn.sigmoid(1.702 * gate_part) * (up_part + 1.0)).astype(jnp.bfloat16)
        summed = jnp.zeros((most, D), jnp.float32)
        for part_index in range(N_TENSOR):
            lower = part_index * hidden_local
            partial_out = jnp.dot(activation[:, lower:lower + hidden_local], w_out[lower:lower + hidden_local], preferred_element_type=jnp.float32)
            summed = summed + lax.optimization_barrier(partial_out.astype(jnp.bfloat16)).astype(jnp.float32)
        result = lax.optimization_barrier(summed.astype(jnp.bfloat16)).astype(jnp.float32)
        accumulated = accumulated.at[member_rows].add(member_weight[:, None] * result)
        return (accumulated, None)
    accumulated, unused = lax.scan(one_expert, jnp.zeros((ROWS, D), jnp.float32), jnp.arange(EXPERTS, dtype=jnp.int32))
    return accumulated

def reference(residual, queries, new_kv, kv_cache, lengths, sink_logits, out_proj, norm_gain, expert_ids, gate_weights, w_gate_up, w_down):
    positions = jnp.arange(CACHE, dtype=jnp.int32)
    cache_valid = positions[None, :] < lengths[:, None]
    results = []
    for step_index in range(STEPS):
        count = step_index + 1
        fresh = new_kv[:count].reshape(count, ROWS, 2, KVH, HD)
        fresh = jnp.transpose(fresh, (2, 1, 3, 0, 4))
        key_all = jnp.concatenate([kv_cache[:, 0], fresh[0]], axis=2)
        value_all = jnp.concatenate([kv_cache[:, 1], fresh[1]], axis=2)
        valid = jnp.concatenate([cache_valid, jnp.ones((ROWS, count), dtype=bool)], axis=1)
        queries_now = queries[step_index].reshape(ROWS, KVH, QH // KVH, HD)
        heads = attend(queries_now, key_all, value_all, valid, sink_logits)
        projected = jnp.dot(heads, out_proj, preferred_element_type=jnp.float32)
        hidden = (residual[step_index].astype(jnp.float32) + projected).astype(jnp.bfloat16)
        widened = lax.optimization_barrier(hidden).astype(jnp.float32)
        inv_rms = lax.rsqrt(lax.optimization_barrier(jnp.mean(widened * widened, axis=1, keepdims=True)) + 1e-05)
        normed = (widened * inv_rms * norm_gain.astype(jnp.float32)).astype(jnp.bfloat16)
        mixture = mixture_of_experts(normed, expert_ids[step_index], gate_weights[step_index], w_gate_up, w_down)
        results.append((widened + mixture).astype(jnp.bfloat16))
    return jnp.stack(results)
```

```python
import jax
import jax.numpy as jnp
from jax import lax
from jax.sharding import PartitionSpec as P

D = 2880
HD = 64
TOP = 4
STEPS = 2
CACHE = 32


def routing_tables(expert_now, weight_now, experts, capacity):
    row_count, top_count = expert_now.shape
    flattened = expert_now.reshape(-1)
    onehot = (flattened[:, None] == jnp.arange(experts, dtype=jnp.int32)[None, :]).astype(jnp.int32)
    earlier = jnp.cumsum(onehot, axis=0) - onehot
    slot_index = flattened * capacity + jnp.sum(earlier * onehot, axis=1)
    matches = slot_index[None, :] == jnp.arange(experts * capacity, dtype=jnp.int32)[:, None]
    matches = matches.reshape(experts * capacity, row_count, top_count)
    scatter_table = jnp.sum(matches.astype(jnp.int32), axis=2).astype(jnp.bfloat16)
    combine_table = jnp.sum(jnp.where(matches, weight_now[None, :, :], 0.0), axis=2).T
    return (scatter_table, combine_table)


def attend_local(queries_now, key_cache, value_cache, fresh_keys, fresh_values, valid, sink_logits):
    factor = HD ** (-0.5)
    cached = (
        jnp.einsum("rkgd,rkjd->rkgj", queries_now, key_cache, preferred_element_type=jnp.float32)
        * factor
    )
    recent = (
        jnp.einsum("rkgd,rkjd->rkgj", queries_now, fresh_keys, preferred_element_type=jnp.float32)
        * factor
    )
    cached = jnp.where(valid[:, None, None, :], cached, -jnp.inf)
    sinks = sink_logits.reshape(1, queries_now.shape[1], queries_now.shape[2], 1)
    peak = jnp.maximum(
        jnp.maximum(jnp.max(cached, axis=3, keepdims=True), jnp.max(recent, axis=3, keepdims=True)),
        sinks,
    )
    cached_weights = jnp.where(valid[:, None, None, :], jnp.exp(cached - peak), 0.0)
    recent_weights = jnp.exp(recent - peak)
    totals = (
        jnp.sum(cached_weights, axis=3, keepdims=True)
        + jnp.sum(recent_weights, axis=3, keepdims=True)
        + jnp.exp(sinks - peak)
    )
    cached_probs = (cached_weights / totals).astype(jnp.bfloat16)
    recent_probs = (recent_weights / totals).astype(jnp.bfloat16)
    mixed = jnp.einsum(
        "rkgj,rkjd->rkgd", cached_probs, value_cache, preferred_element_type=jnp.float32
    )
    mixed = mixed + jnp.einsum(
        "rkgj,rkjd->rkgd", recent_probs, fresh_values, preferred_element_type=jnp.float32
    )
    return mixed.astype(jnp.bfloat16).reshape(queries_now.shape[0], -1)


def body_compact(
    residual,
    queries,
    new_kv,
    kv_cache,
    lengths,
    sink_logits,
    out_proj,
    norm_gain,
    expert_ids,
    gate_weights,
    w_gate_up,
    w_down,
):
    row_count = residual.shape[1]
    own_width = residual.shape[2]
    experts = lax.axis_size("expert")
    tensor_rank = lax.axis_index("tensor")
    capacity = min(row_count, 2 * row_count * TOP // experts)
    kv_local = kv_cache.shape[2]
    group_size = queries.shape[2] // (HD * kv_local)
    hidden_local = w_down.shape[1]
    w_in = w_gate_up.reshape(D, 2 * hidden_local)
    w_out = w_down.reshape(hidden_local, D)
    col_start = tensor_rank * own_width
    gain_wide = norm_gain.astype(jnp.float32)
    valid = jnp.arange(CACHE, dtype=jnp.int32)[None, :] < lengths[:, None]
    results = []
    for step_index in range(STEPS):
        count = step_index + 1
        fresh = new_kv[:count].reshape(count, row_count, 2, kv_local, HD).transpose(2, 1, 3, 0, 4)
        queries_now = queries[step_index].reshape(row_count, kv_local, group_size, HD)
        heads = attend_local(
            queries_now, kv_cache[:, 0], kv_cache[:, 1], fresh[0], fresh[1], valid, sink_logits
        )
        projected = jnp.dot(heads, out_proj, preferred_element_type=jnp.float32)
        own_cols = lax.dynamic_slice_in_dim(projected, col_start, own_width, 1) + residual[
            step_index
        ].astype(jnp.float32)
        with_input = lax.dynamic_update_slice_in_dim(projected, own_cols, col_start, 1)
        scatter_table, combine_table = routing_tables(
            expert_ids[step_index], gate_weights[step_index], experts, capacity
        )
        hidden_full = lax.psum(with_input, "tensor").astype(jnp.bfloat16)
        widened = lax.optimization_barrier(hidden_full).astype(jnp.float32)
        inv_rms = lax.rsqrt(jnp.mean(widened * widened, axis=1, keepdims=True) + 1e-05)
        normed = (widened * inv_rms * gain_wide).astype(jnp.bfloat16)
        hidden_own = lax.dynamic_slice_in_dim(hidden_full, col_start, own_width, 1)
        outgoing = jnp.dot(scatter_table, normed, preferred_element_type=jnp.float32).astype(
            jnp.bfloat16
        )
        outgoing = outgoing.reshape(experts, capacity, D)
        received = lax.all_to_all(outgoing, "expert", split_axis=0, concat_axis=0, tiled=True)
        run_count = received.shape[1]
        gate_up = jnp.dot(
            received.reshape(-1, D), w_in, preferred_element_type=jnp.float32
        ).reshape(-1, 2, hidden_local)
        gate_part = gate_up[:, 0, :]
        up_part = gate_up[:, 1, :]
        activation = (gate_part * jax.nn.sigmoid(1.702 * gate_part) * (up_part + 1.0)).astype(
            jnp.bfloat16
        )
        run_partial_out = jnp.dot(activation, w_out, preferred_element_type=jnp.float32)
        summed = lax.psum_scatter(
            run_partial_out.reshape(received.shape[0], run_count, D).astype(jnp.bfloat16),
            "tensor",
            scatter_dimension=2,
            tiled=True,
        )
        returned = lax.all_to_all(summed, "expert", split_axis=0, concat_axis=0, tiled=True)
        returned_wide = returned.reshape(experts * capacity, own_width).astype(jnp.float32)
        mixture = jnp.dot(combine_table, returned_wide, precision=lax.Precision.HIGHEST)
        results.append((hidden_own.astype(jnp.float32) + mixture).astype(jnp.bfloat16))
    return jnp.stack(results)


def attend_steps(queries, new_kv, kv_cache, valid, sink_logits):
    row_count, kv_local = kv_cache.shape[0], kv_cache.shape[2]
    group_size = queries.shape[2] // (HD * kv_local)
    fresh = new_kv.reshape(STEPS, row_count, 2, kv_local, HD).transpose(2, 1, 3, 0, 4)
    key_all = jnp.concatenate([kv_cache[:, 0], fresh[0]], axis=2)
    value_all = jnp.concatenate([kv_cache[:, 1], fresh[1]], axis=2)
    asked = queries.reshape(STEPS, row_count, kv_local, group_size, HD)
    asked = asked.transpose(1, 2, 0, 3, 4).reshape(row_count, kv_local, STEPS * group_size, HD)
    step_of = jnp.arange(STEPS * group_size, dtype=jnp.int32) // group_size
    seen_new = jnp.arange(STEPS, dtype=jnp.int32)[None, :] <= step_of[:, None]
    seen = jnp.concatenate(
        [
            jnp.broadcast_to(valid[:, None, :], (row_count, STEPS * group_size, CACHE)),
            jnp.broadcast_to(seen_new[None], (row_count, STEPS * group_size, STEPS)),
        ],
        axis=2,
    )[:, None]
    scores = jnp.einsum("rkgd,rkjd->rkgj", asked, key_all, preferred_element_type=jnp.float32)
    scores = jnp.where(seen, scores * HD ** (-0.5), -jnp.inf)
    sinks = jnp.tile(sink_logits.reshape(kv_local, group_size), (1, STEPS))[None, :, :, None]
    peak = jnp.maximum(jnp.max(scores, axis=3, keepdims=True), sinks)
    weights = jnp.exp(scores - peak)
    totals = jnp.sum(weights, axis=3, keepdims=True) + jnp.exp(sinks - peak)
    probs = (weights / totals).astype(jnp.bfloat16)
    mixed = jnp.einsum("rkgj,rkjd->rkgd", probs, value_all, preferred_element_type=jnp.float32)
    mixed = mixed.astype(jnp.bfloat16).reshape(row_count, kv_local, STEPS, group_size, HD)
    return mixed.transpose(2, 0, 1, 3, 4).reshape(STEPS * row_count, -1)


def body_dense(
    residual,
    queries,
    new_kv,
    kv_cache,
    lengths,
    sink_logits,
    out_proj,
    norm_gain,
    expert_ids,
    gate_weights,
    w_gate_up,
    w_down,
):
    row_count, own_width = residual.shape[1:]
    experts = lax.axis_size("expert")
    both = STEPS * row_count
    hidden_local = w_down.shape[1]
    col_start = lax.axis_index("tensor") * own_width
    valid = jnp.arange(CACHE, dtype=jnp.int32)[None, :] < lengths[:, None]
    heads = attend_steps(queries, new_kv, kv_cache, valid, sink_logits)
    projected = jnp.dot(heads, out_proj, preferred_element_type=jnp.float32)
    own_cols = lax.dynamic_slice_in_dim(projected, col_start, own_width, 1)
    own_cols = own_cols + residual.reshape(both, own_width).astype(jnp.float32)
    with_input = lax.dynamic_update_slice_in_dim(projected, own_cols, col_start, 1)
    hidden_full = lax.psum(with_input, "tensor").astype(jnp.bfloat16)
    widened = lax.optimization_barrier(hidden_full).astype(jnp.float32)
    inv_rms = lax.rsqrt(jnp.mean(widened * widened, axis=1, keepdims=True) + 1e-05)
    normed = (widened * inv_rms * norm_gain.astype(jnp.float32)).astype(jnp.bfloat16)
    hidden_own = lax.dynamic_slice_in_dim(hidden_full, col_start, own_width, 1)
    gathered = lax.all_gather(normed, "expert", axis=0, tiled=True)
    w_in = w_gate_up.reshape(2 * D, hidden_local)
    twice = jnp.repeat(gathered, 2, axis=1)
    even = jnp.arange(2 * D, dtype=jnp.int32)[None, :] % 2 == 0
    placed = jnp.concatenate([jnp.where(even, twice, 0), jnp.where(even, 0, twice)], axis=0)
    gate_up = jnp.dot(placed, w_in, preferred_element_type=jnp.float32)
    gate_part, up_part = gate_up[: experts * both], gate_up[experts * both :]
    activation = (gate_part * jax.nn.sigmoid(1.702 * gate_part) * (up_part + 1.0)).astype(
        jnp.bfloat16
    )
    partial_out = jnp.dot(activation, w_down[0], preferred_element_type=jnp.float32)
    partial_out = partial_out.astype(jnp.bfloat16)
    kept = lax.dynamic_slice_in_dim(partial_out, col_start, own_width, 1)
    given = lax.dynamic_slice_in_dim(partial_out, own_width - col_start, own_width, 1)
    got = lax.ppermute(given, "tensor", [(0, 1), (1, 0)])
    summed = (kept.astype(jnp.float32) + got.astype(jnp.float32)).astype(jnp.bfloat16)
    returned = lax.all_to_all(
        summed.reshape(experts, both, own_width), "expert", split_axis=0, concat_axis=0, tiled=True
    )
    named = expert_ids[..., None] == jnp.arange(experts, dtype=jnp.int32)
    share = jnp.sum(jnp.where(named, gate_weights[..., None], 0.0), axis=2).reshape(both, experts)
    mixture = jnp.sum(returned.astype(jnp.float32) * share.T[:, :, None], axis=0)
    out = (hidden_own.astype(jnp.float32) + mixture).astype(jnp.bfloat16)
    return out.reshape(STEPS, row_count, own_width)


def body(residual, *rest):
    row_count, experts = residual.shape[1], lax.axis_size("expert")
    compact = 2 * row_count * TOP // experts < row_count
    return (body_compact if compact else body_dense)(residual, *rest)


def solution(mesh):
    in_specs = (
        P(None, ("groups", "expert"), "tensor"),
        P(None, ("groups", "expert"), "tensor"),
        P(None, ("groups", "expert"), None, "tensor"),
        P(("groups", "expert"), None, "tensor", None, None),
        P(("groups", "expert")),
        P("tensor"),
        P("tensor", None),
        P(),
        P(None, ("groups", "expert"), None),
        P(None, ("groups", "expert"), None),
        P("expert", None, None, "tensor"),
        P("expert", "tensor", None),
    )
    out_specs = P(None, ("groups", "expert"), "tensor")
    return jax.shard_map(body, mesh=mesh, in_specs=in_specs, out_specs=out_specs, check_vma=False)
```

```python
import functools
import jax
import jax.numpy as jnp
from jax import lax
from jax.experimental import pallas as pl
from jax.experimental.pallas import tpu as pltpu
from jax.sharding import PartitionSpec as P

D = 2880
HD = 64
TOP = 4
STEPS = 2
CACHE = 32


def routing_tables(expert_now, weight_now, experts, capacity):
    row_count, top_count = expert_now.shape
    flattened = expert_now.reshape(-1)
    onehot = (flattened[:, None] == jnp.arange(experts, dtype=jnp.int32)[None, :]).astype(jnp.int32)
    earlier = jnp.cumsum(onehot, axis=0) - onehot
    slot_index = flattened * capacity + jnp.sum(earlier * onehot, axis=1)
    matches = slot_index[None, :] == jnp.arange(experts * capacity, dtype=jnp.int32)[:, None]
    matches = matches.reshape(experts * capacity, row_count, top_count)
    scatter_table = jnp.sum(matches.astype(jnp.int32), axis=2).astype(jnp.bfloat16)
    combine_table = jnp.sum(jnp.where(matches, weight_now[None, :, :], 0.0), axis=2).T
    return (scatter_table, combine_table)


def attend_local(queries_now, key_cache, value_cache, fresh_keys, fresh_values, valid, sink_logits):
    factor = HD ** (-0.5)
    cached = (
        jnp.einsum("rkgd,rkjd->rkgj", queries_now, key_cache, preferred_element_type=jnp.float32)
        * factor
    )
    recent = (
        jnp.einsum("rkgd,rkjd->rkgj", queries_now, fresh_keys, preferred_element_type=jnp.float32)
        * factor
    )
    cached = jnp.where(valid[:, None, None, :], cached, -jnp.inf)
    sinks = sink_logits.reshape(1, queries_now.shape[1], queries_now.shape[2], 1)
    peak = jnp.maximum(
        jnp.maximum(jnp.max(cached, axis=3, keepdims=True), jnp.max(recent, axis=3, keepdims=True)),
        sinks,
    )
    cached_weights = jnp.where(valid[:, None, None, :], jnp.exp(cached - peak), 0.0)
    recent_weights = jnp.exp(recent - peak)
    totals = (
        jnp.sum(cached_weights, axis=3, keepdims=True)
        + jnp.sum(recent_weights, axis=3, keepdims=True)
        + jnp.exp(sinks - peak)
    )
    cached_probs = (cached_weights / totals).astype(jnp.bfloat16)
    recent_probs = (recent_weights / totals).astype(jnp.bfloat16)
    mixed = jnp.einsum(
        "rkgj,rkjd->rkgd", cached_probs, value_cache, preferred_element_type=jnp.float32
    )
    mixed = mixed + jnp.einsum(
        "rkgj,rkjd->rkgd", recent_probs, fresh_values, preferred_element_type=jnp.float32
    )
    return mixed.astype(jnp.bfloat16).reshape(queries_now.shape[0], -1)


def body_compact(
    residual,
    queries,
    new_kv,
    kv_cache,
    lengths,
    sink_logits,
    out_proj,
    norm_gain,
    expert_ids,
    gate_weights,
    w_gate_up,
    w_down,
):
    row_count = residual.shape[1]
    own_width = residual.shape[2]
    experts = lax.axis_size("expert")
    tensor_rank = lax.axis_index("tensor")
    capacity = min(row_count, 2 * row_count * TOP // experts)
    kv_local = kv_cache.shape[2]
    group_size = queries.shape[2] // (HD * kv_local)
    hidden_local = w_down.shape[1]
    w_in = w_gate_up.reshape(D, 2 * hidden_local)
    w_out = w_down.reshape(hidden_local, D)
    col_start = tensor_rank * own_width
    gain_wide = norm_gain.astype(jnp.float32)
    valid = jnp.arange(CACHE, dtype=jnp.int32)[None, :] < lengths[:, None]
    results = []
    for step_index in range(STEPS):
        count = step_index + 1
        fresh = new_kv[:count].reshape(count, row_count, 2, kv_local, HD).transpose(2, 1, 3, 0, 4)
        queries_now = queries[step_index].reshape(row_count, kv_local, group_size, HD)
        heads = attend_local(
            queries_now, kv_cache[:, 0], kv_cache[:, 1], fresh[0], fresh[1], valid, sink_logits
        )
        projected = jnp.dot(heads, out_proj, preferred_element_type=jnp.float32)
        own_cols = lax.dynamic_slice_in_dim(projected, col_start, own_width, 1) + residual[
            step_index
        ].astype(jnp.float32)
        with_input = lax.dynamic_update_slice_in_dim(projected, own_cols, col_start, 1)
        scatter_table, combine_table = routing_tables(
            expert_ids[step_index], gate_weights[step_index], experts, capacity
        )
        hidden_full = lax.psum(with_input, "tensor").astype(jnp.bfloat16)
        widened = lax.optimization_barrier(hidden_full).astype(jnp.float32)
        inv_rms = lax.rsqrt(jnp.mean(widened * widened, axis=1, keepdims=True) + 1e-05)
        normed = (widened * inv_rms * gain_wide).astype(jnp.bfloat16)
        hidden_own = lax.dynamic_slice_in_dim(hidden_full, col_start, own_width, 1)
        outgoing = jnp.dot(scatter_table, normed, preferred_element_type=jnp.float32).astype(
            jnp.bfloat16
        )
        outgoing = outgoing.reshape(experts, capacity, D)
        received = lax.all_to_all(outgoing, "expert", split_axis=0, concat_axis=0, tiled=True)
        run_count = received.shape[1]
        gate_up = jnp.dot(
            received.reshape(-1, D), w_in, preferred_element_type=jnp.float32
        ).reshape(-1, 2, hidden_local)
        gate_part = gate_up[:, 0, :]
        up_part = gate_up[:, 1, :]
        activation = (gate_part * jax.nn.sigmoid(1.702 * gate_part) * (up_part + 1.0)).astype(
            jnp.bfloat16
        )
        run_partial_out = jnp.dot(activation, w_out, preferred_element_type=jnp.float32)
        summed = lax.psum_scatter(
            run_partial_out.reshape(received.shape[0], run_count, D).astype(jnp.bfloat16),
            "tensor",
            scatter_dimension=2,
            tiled=True,
        )
        returned = lax.all_to_all(summed, "expert", split_axis=0, concat_axis=0, tiled=True)
        returned_wide = returned.reshape(experts * capacity, own_width).astype(jnp.float32)
        mixture = jnp.dot(combine_table, returned_wide, precision=lax.Precision.HIGHEST)
        results.append((hidden_own.astype(jnp.float32) + mixture).astype(jnp.bfloat16))
    return jnp.stack(results)


def attend_steps(queries, new_kv, kv_cache, valid, sink_logits):
    row_count, kv_local = kv_cache.shape[0], kv_cache.shape[2]
    group_size = queries.shape[2] // (HD * kv_local)
    fresh = new_kv.reshape(STEPS, row_count, 2, kv_local, HD).transpose(2, 1, 3, 0, 4)
    key_all = jnp.concatenate([kv_cache[:, 0], fresh[0]], axis=2)
    value_all = jnp.concatenate([kv_cache[:, 1], fresh[1]], axis=2)
    asked = queries.reshape(STEPS, row_count, kv_local, group_size, HD)
    asked = asked.transpose(1, 2, 0, 3, 4).reshape(row_count, kv_local, STEPS * group_size, HD)
    step_of = jnp.arange(STEPS * group_size, dtype=jnp.int32) // group_size
    seen_new = jnp.arange(STEPS, dtype=jnp.int32)[None, :] <= step_of[:, None]
    seen = jnp.concatenate(
        [
            jnp.broadcast_to(valid[:, None, :], (row_count, STEPS * group_size, CACHE)),
            jnp.broadcast_to(seen_new[None], (row_count, STEPS * group_size, STEPS)),
        ],
        axis=2,
    )[:, None]
    scores = jnp.einsum("rkgd,rkjd->rkgj", asked, key_all, preferred_element_type=jnp.float32)
    scores = jnp.where(seen, scores * HD ** (-0.5), -jnp.inf)
    sinks = jnp.tile(sink_logits.reshape(kv_local, group_size), (1, STEPS))[None, :, :, None]
    peak = jnp.maximum(jnp.max(scores, axis=3, keepdims=True), sinks)
    weights = jnp.exp(scores - peak)
    totals = jnp.sum(weights, axis=3, keepdims=True) + jnp.exp(sinks - peak)
    probs = (weights / totals).astype(jnp.bfloat16)
    mixed = jnp.einsum("rkgj,rkjd->rkgd", probs, value_all, preferred_element_type=jnp.float32)
    mixed = mixed.astype(jnp.bfloat16).reshape(row_count, kv_local, STEPS, group_size, HD)
    return mixed.transpose(2, 0, 1, 3, 4).reshape(STEPS * row_count, -1)


WIDE = 3072
HALF = WIDE // 2
LANES = 128
SHARE_AT = WIDE - LANES
PAIRS = 192


def expert_kernel(
    zs,
    experts,
    rows_ref,
    hidden_ref,
    w_in_hbm,
    w_down_hbm,
    out_ref,
    w_in,
    w_down,
    w_gate,
    w_up,
    w_half,
    slots,
    act,
    kept,
    sib_out,
    sib_in,
    x_out,
    x_in,
    z_out,
    z_in,
    load_sem,
    own_send,
    own_recv,
    pass_send,
    core_send,
    core_recv,
    sib_send,
    sib_recv,
    xs_send,
    xs_recv,
    zs_send,
    zs_recv,
):
    group, me, core = lax.axis_index("groups"), lax.axis_index("expert"), lax.axis_index("tensor")
    z, x = me // 2, me % 2
    own_width = out_ref.shape[1]
    both = rows_ref.shape[0]
    width = 2 * own_width
    hidden_local = w_gate.shape[1]

    def device(to_z, to_x, to_core):
        return (group, to_z * 2 + to_x, to_core)

    peers = [device(lax.rem(z + d, zs), x, core) for d in range(1, zs)]
    other_x = device(z, 1 - x, core)
    other_core = device(z, x, 1 - core)
    barrier = pltpu.get_barrier_semaphore()
    for peer in peers + [other_x, other_core]:
        pl.semaphore_signal(barrier, inc=1, device_id=peer, device_id_type=pl.DeviceIdType.MESH)
    load_in = pltpu.make_async_copy(w_in_hbm, w_in, load_sem.at[0])
    load_in.start()
    load_down = pltpu.make_async_copy(w_down_hbm, w_down, load_sem.at[1])
    load_down.start()
    mine = x * zs + z
    slots[mine] = rows_ref[...]
    pl.semaphore_wait(barrier, zs + 1)

    def remote(src, dst, send, recv, to):
        return pltpu.make_async_remote_copy(
            src_ref=src,
            dst_ref=dst,
            send_sem=send,
            recv_sem=recv,
            device_id=to,
            device_id_type=pl.DeviceIdType.MESH,
        )

    def part(slot, half):
        return slots.at[slot, :, pl.ds(pl.multiple_of(half * HALF, HALF), HALF)]

    started = []

    def spread(slot, send, recv, to):
        copy = remote(part(slot, core), part(slot, core), send, recv.at[slot], to)
        copy.start()
        started.append(copy)

    def arrived(slot, half, recv):
        remote(part(slot, half), part(slot, half), own_send.at[0], recv.at[slot], other_x).wait_recv()

    spread(mine, own_send.at[0], own_recv, other_x)
    for d in range(1, zs):
        spread(mine, own_send.at[d], own_recv, peers[d - 1])

    row = lax.broadcasted_iota(jnp.int32, (PAIRS, 2 * PAIRS), 0)
    column = lax.broadcasted_iota(jnp.int32, (PAIRS, 2 * PAIRS), 1)
    evens = jnp.where(column == 2 * row, 1.0, 0.0).astype(jnp.bfloat16)
    odds = jnp.where(column == 2 * row + 1, 1.0, 0.0).astype(jnp.bfloat16)

    def separate(start, stop):
        def one(i, carry):
            block = w_in[pl.ds(pl.multiple_of(i * 2 * PAIRS, 2 * PAIRS), 2 * PAIRS), :]
            at = pl.ds(pl.multiple_of(i * PAIRS, PAIRS), PAIRS)
            w_gate[at, :] = jnp.dot(evens, block, preferred_element_type=jnp.float32).astype(
                jnp.bfloat16
            )
            w_up[at, :] = jnp.dot(odds, block, preferred_element_type=jnp.float32).astype(
                jnp.bfloat16
            )
            return carry

        lax.fori_loop(start, stop, one, 0)

    blocks = width // PAIRS
    load_in.wait()
    for d in range(1, zs):
        separate(blocks * (d - 1) // (zs - 1), blocks * d // (zs - 1))
        slot = x * zs + lax.rem(z + zs - d, zs)
        arrived(slot, core, own_recv)
        spread(slot, pass_send.at[d], own_recv, other_x)
        spread(slot, core_send.at[d], core_recv, other_core)
    load_down.wait()

    def widen(i, carry):
        at = pl.ds(pl.multiple_of(i * 96, 96), 96)
        zeros = jnp.zeros((96, HALF - own_width), jnp.bfloat16)
        w_half[0, at, :] = jnp.concatenate([w_down[at, :own_width], zeros], axis=1)
        w_half[1, at, :] = jnp.concatenate([w_down[at, own_width:], zeros], axis=1)
        return carry

    lax.fori_loop(0, hidden_local // 96, widen, 0)

    def first(side, at_x):
        def one(c, carry):
            at = pl.ds(pl.multiple_of(c * 256, 256), 256)
            inputs = slots[pl.ds(at_x * zs, zs), :, :width].reshape(zs * both, width)
            gate = jnp.dot(inputs, w_gate[:, at], preferred_element_type=jnp.float32)
            up = jnp.dot(inputs, w_up[:, at], preferred_element_type=jnp.float32)
            value = gate * jax.nn.sigmoid(1.702 * gate) * (up + 1.0)
            act[side, :, at] = value.astype(jnp.bfloat16)
            return carry

        lax.fori_loop(0, hidden_local // 256, one, 0)

    for d in range(1, zs):
        arrived(x * zs + lax.rem(z + zs - d, zs), 1 - core, core_recv)
    first(0, x)
    for d in range(zs):
        slot = (1 - x) * zs + lax.rem(z + zs - d, zs)
        arrived(slot, core, own_recv)
        spread(slot, core_send.at[zs + d], core_recv, other_core)
    for d in range(zs):
        arrived((1 - x) * zs + lax.rem(z + zs - d, zs), 1 - core, core_recv)
    first(1, 1 - x)

    def second(side, at_x):
        lane = lax.broadcasted_iota(jnp.int32, (1, LANES), 1)
        taken = (lax.rem(lane, experts) == me) & (lane < 3 * experts)
        shares = slots[pl.ds(at_x * zs, zs), :, SHARE_AT:].reshape(zs * both, LANES)
        share = jnp.sum(jnp.where(taken, shares.astype(jnp.float32), 0.0), axis=1, keepdims=True)

        def tile(c, carry):
            at = pl.ds(pl.multiple_of(c * 512, 512), 512)
            given = jnp.dot(act[side], w_half[1 - core, :, at], preferred_element_type=jnp.float32)
            given = (given * share).astype(jnp.bfloat16)
            sib_out[side, :, :, at] = given.reshape(zs, both, 512)
            return carry

        def own_tile(c, carry):
            at = pl.ds(pl.multiple_of(c * 512, 512), 512)
            own = jnp.dot(act[side], w_half[core, :, at], preferred_element_type=jnp.float32)
            kept[side, :, :, at] = (own * share).reshape(zs, both, 512)
            return carry

        lax.fori_loop(0, HALF // 512, tile, 0)
        copy = remote(
            sib_out.at[side], sib_in.at[side], sib_send.at[side], sib_recv.at[side], other_core
        )
        copy.start()
        lax.fori_loop(0, HALF // 512, own_tile, 0)
        return copy

    across = second(1, 1 - x)
    across.wait_recv()
    started.append(across)
    x_copies = []
    for d in range(zs):
        to_z = lax.rem(z + d + 1, zs)
        x_out[d] = (kept[1, to_z] + sib_in[1, to_z].astype(jnp.float32)).astype(jnp.bfloat16)
        copy = remote(x_out.at[d], x_in.at[d], xs_send.at[d], xs_recv.at[d], other_x)
        copy.start()
        x_copies.append(copy)
        started.append(copy)
    along = second(0, x)
    along.wait_recv()
    started.append(along)
    z_copies = []
    for d in range(zs):
        to_z = lax.rem(z + d + 1, zs)
        x_copies[d].wait_recv()
        total = kept[0, to_z] + sib_in[0, to_z].astype(jnp.float32) + x_in[d].astype(jnp.float32)
        if d < zs - 1:
            z_out[d] = total.astype(jnp.bfloat16)
            copy = remote(z_out.at[d], z_in.at[d], zs_send.at[d], zs_recv.at[d], peers[d])
            copy.start()
            z_copies.append(copy)
            started.append(copy)
    for d in range(zs - 1):
        z_copies[d].wait_recv()
        total = total + z_in[d].astype(jnp.float32)
    out_ref[...] = (hidden_ref[...].astype(jnp.float32) + total[:, :own_width]).astype(
        out_ref.dtype
    )
    for copy in started:
        copy.wait_send()


def run_experts(rows, hidden_own, w_in, w_down, experts):
    both, own_width = hidden_own.shape
    zs = experts // 2
    hidden_local, width = w_down.shape
    bf16, dma = jnp.bfloat16, pltpu.SemaphoreType.DMA
    vmem = pl.BlockSpec(memory_space=pltpu.VMEM)
    anywhere = pl.BlockSpec(memory_space=pl.ANY)
    return pl.pallas_call(
        functools.partial(expert_kernel, zs, experts),
        out_shape=jax.ShapeDtypeStruct((both, own_width), bf16),
        in_specs=[vmem, vmem, anywhere, anywhere],
        out_specs=vmem,
        scratch_shapes=[
            pltpu.VMEM(w_in.shape, bf16),
            pltpu.VMEM(w_down.shape, bf16),
            pltpu.VMEM((width, hidden_local), bf16),
            pltpu.VMEM((width, hidden_local), bf16),
            pltpu.VMEM((2, hidden_local, HALF), bf16),
            pltpu.VMEM((experts, both, WIDE), bf16),
            pltpu.VMEM((2, zs * both, hidden_local), bf16),
            pltpu.VMEM((2, zs, both, HALF), jnp.float32),
            pltpu.VMEM((2, zs, both, HALF), bf16),
            pltpu.VMEM((2, zs, both, HALF), bf16),
            pltpu.VMEM((zs, both, HALF), bf16),
            pltpu.VMEM((zs, both, HALF), bf16),
            pltpu.VMEM((zs - 1, both, HALF), bf16),
            pltpu.VMEM((zs - 1, both, HALF), bf16),
            dma((2,)),
            dma((zs,)),
            dma((experts,)),
            dma((zs,)),
            dma((experts,)),
            dma((experts,)),
            dma((2,)),
            dma((2,)),
            dma((zs,)),
            dma((zs,)),
            dma((zs - 1,)),
            dma((zs - 1,)),
        ],
        compiler_params=pltpu.CompilerParams(
            collective_id=0, has_side_effects=True, vmem_limit_bytes=56 * 2**20
        ),
        cost_estimate=pl.CostEstimate(
            flops=6 * experts * both * width * hidden_local,
            bytes_accessed=14 * 2**20,
            transcendentals=0,
        ),
    )(rows, hidden_own, w_in, w_down)


def body_dense(
    residual,
    queries,
    new_kv,
    kv_cache,
    lengths,
    sink_logits,
    out_proj,
    norm_gain,
    expert_ids,
    gate_weights,
    w_gate_up,
    w_down,
):
    row_count, own_width = residual.shape[1:]
    experts = lax.axis_size("expert")
    both = STEPS * row_count
    hidden_local = w_down.shape[1]
    col_start = lax.axis_index("tensor") * own_width
    valid = jnp.arange(CACHE, dtype=jnp.int32)[None, :] < lengths[:, None]
    heads = attend_steps(queries, new_kv, kv_cache, valid, sink_logits)
    projected = jnp.dot(heads, out_proj, preferred_element_type=jnp.float32)
    own_cols = lax.dynamic_slice_in_dim(projected, col_start, own_width, 1)
    own_cols = own_cols + residual.reshape(both, own_width).astype(jnp.float32)
    with_input = lax.dynamic_update_slice_in_dim(projected, own_cols, col_start, 1)
    hidden_full = lax.psum(with_input, "tensor").astype(jnp.bfloat16)
    widened = lax.optimization_barrier(hidden_full).astype(jnp.float32)
    inv_rms = lax.rsqrt(jnp.mean(widened * widened, axis=1, keepdims=True) + 1e-05)
    normed = (widened * inv_rms * norm_gain.astype(jnp.float32)).astype(jnp.bfloat16)
    hidden_own = lax.dynamic_slice_in_dim(hidden_full, col_start, own_width, 1)
    named = expert_ids[..., None] == jnp.arange(experts, dtype=jnp.int32)
    share = jnp.sum(jnp.where(named, gate_weights[..., None], 0.0), axis=2).reshape(both, experts)
    pieces = []
    for unused in range(3):
        piece = lax.reduce_precision(share, 8, 7)
        pieces.append(piece.astype(jnp.bfloat16))
        share = share - piece
    rows = jnp.concatenate([normed, jnp.zeros((both, SHARE_AT - D), jnp.bfloat16)] + pieces, axis=1)
    rows = jnp.pad(rows, ((0, 0), (0, WIDE - rows.shape[1])))
    out = run_experts(
        rows, hidden_own, w_gate_up.reshape(2 * D, hidden_local), w_down[0], experts
    )
    return out.reshape(STEPS, row_count, own_width)


def body(residual, *rest):
    row_count, experts = residual.shape[1], lax.axis_size("expert")
    compact = 2 * row_count * TOP // experts < row_count
    return (body_compact if compact else body_dense)(residual, *rest)


def solution(mesh):
    in_specs = (
        P(None, ("groups", "expert"), "tensor"),
        P(None, ("groups", "expert"), "tensor"),
        P(None, ("groups", "expert"), None, "tensor"),
        P(("groups", "expert"), None, "tensor", None, None),
        P(("groups", "expert")),
        P("tensor"),
        P("tensor", None),
        P(),
        P(None, ("groups", "expert"), None),
        P(None, ("groups", "expert"), None),
        P("expert", None, None, "tensor"),
        P("expert", "tensor", None),
    )
    out_specs = P(None, ("groups", "expert"), "tensor")
    return jax.shard_map(body, mesh=mesh, in_specs=in_specs, out_specs=out_specs, check_vma=False)
```

```python
import functools
import jax
import jax.numpy as jnp
from jax import lax
from jax.experimental import pallas as pl
from jax.experimental.pallas import tpu as pltpu
from jax.sharding import PartitionSpec as P

D = 2880
HD = 64
TOP = 4
STEPS = 2
CACHE = 32


def routing_tables(expert_now, weight_now, experts, capacity):
    row_count, top_count = expert_now.shape
    flattened = expert_now.reshape(-1)
    onehot = (flattened[:, None] == jnp.arange(experts, dtype=jnp.int32)[None, :]).astype(jnp.int32)
    earlier = jnp.cumsum(onehot, axis=0) - onehot
    slot_index = flattened * capacity + jnp.sum(earlier * onehot, axis=1)
    matches = slot_index[None, :] == jnp.arange(experts * capacity, dtype=jnp.int32)[:, None]
    matches = matches.reshape(experts * capacity, row_count, top_count)
    scatter_table = jnp.sum(matches.astype(jnp.int32), axis=2).astype(jnp.bfloat16)
    combine_table = jnp.sum(jnp.where(matches, weight_now[None, :, :], 0.0), axis=2).T
    return (scatter_table, combine_table)


def attend_local(queries_now, key_cache, value_cache, fresh_keys, fresh_values, valid, sink_logits):
    factor = HD ** (-0.5)
    cached = (
        jnp.einsum("rkgd,rkjd->rkgj", queries_now, key_cache, preferred_element_type=jnp.float32)
        * factor
    )
    recent = (
        jnp.einsum("rkgd,rkjd->rkgj", queries_now, fresh_keys, preferred_element_type=jnp.float32)
        * factor
    )
    cached = jnp.where(valid[:, None, None, :], cached, -jnp.inf)
    sinks = sink_logits.reshape(1, queries_now.shape[1], queries_now.shape[2], 1)
    peak = jnp.maximum(
        jnp.maximum(jnp.max(cached, axis=3, keepdims=True), jnp.max(recent, axis=3, keepdims=True)),
        sinks,
    )
    cached_weights = jnp.where(valid[:, None, None, :], jnp.exp(cached - peak), 0.0)
    recent_weights = jnp.exp(recent - peak)
    totals = (
        jnp.sum(cached_weights, axis=3, keepdims=True)
        + jnp.sum(recent_weights, axis=3, keepdims=True)
        + jnp.exp(sinks - peak)
    )
    cached_probs = (cached_weights / totals).astype(jnp.bfloat16)
    recent_probs = (recent_weights / totals).astype(jnp.bfloat16)
    mixed = jnp.einsum(
        "rkgj,rkjd->rkgd", cached_probs, value_cache, preferred_element_type=jnp.float32
    )
    mixed = mixed + jnp.einsum(
        "rkgj,rkjd->rkgd", recent_probs, fresh_values, preferred_element_type=jnp.float32
    )
    return mixed.astype(jnp.bfloat16).reshape(queries_now.shape[0], -1)


def body_compact(
    residual,
    queries,
    new_kv,
    kv_cache,
    lengths,
    sink_logits,
    out_proj,
    norm_gain,
    expert_ids,
    gate_weights,
    w_gate_up,
    w_down,
):
    row_count = residual.shape[1]
    own_width = residual.shape[2]
    experts = lax.axis_size("expert")
    tensor_rank = lax.axis_index("tensor")
    capacity = min(row_count, 2 * row_count * TOP // experts)
    kv_local = kv_cache.shape[2]
    group_size = queries.shape[2] // (HD * kv_local)
    hidden_local = w_down.shape[1]
    w_in = w_gate_up.reshape(D, 2 * hidden_local)
    w_out = w_down.reshape(hidden_local, D)
    col_start = tensor_rank * own_width
    gain_wide = norm_gain.astype(jnp.float32)
    valid = jnp.arange(CACHE, dtype=jnp.int32)[None, :] < lengths[:, None]
    results = []
    for step_index in range(STEPS):
        count = step_index + 1
        fresh = new_kv[:count].reshape(count, row_count, 2, kv_local, HD).transpose(2, 1, 3, 0, 4)
        queries_now = queries[step_index].reshape(row_count, kv_local, group_size, HD)
        heads = attend_local(
            queries_now, kv_cache[:, 0], kv_cache[:, 1], fresh[0], fresh[1], valid, sink_logits
        )
        projected = jnp.dot(heads, out_proj, preferred_element_type=jnp.float32)
        own_cols = lax.dynamic_slice_in_dim(projected, col_start, own_width, 1) + residual[
            step_index
        ].astype(jnp.float32)
        with_input = lax.dynamic_update_slice_in_dim(projected, own_cols, col_start, 1)
        scatter_table, combine_table = routing_tables(
            expert_ids[step_index], gate_weights[step_index], experts, capacity
        )
        hidden_full = lax.psum(with_input, "tensor").astype(jnp.bfloat16)
        widened = lax.optimization_barrier(hidden_full).astype(jnp.float32)
        inv_rms = lax.rsqrt(jnp.mean(widened * widened, axis=1, keepdims=True) + 1e-05)
        normed = (widened * inv_rms * gain_wide).astype(jnp.bfloat16)
        hidden_own = lax.dynamic_slice_in_dim(hidden_full, col_start, own_width, 1)
        outgoing = jnp.dot(scatter_table, normed, preferred_element_type=jnp.float32).astype(
            jnp.bfloat16
        )
        outgoing = outgoing.reshape(experts, capacity, D)
        received = lax.all_to_all(outgoing, "expert", split_axis=0, concat_axis=0, tiled=True)
        run_count = received.shape[1]
        gate_up = jnp.dot(
            received.reshape(-1, D), w_in, preferred_element_type=jnp.float32
        ).reshape(-1, 2, hidden_local)
        gate_part = gate_up[:, 0, :]
        up_part = gate_up[:, 1, :]
        activation = (gate_part * jax.nn.sigmoid(1.702 * gate_part) * (up_part + 1.0)).astype(
            jnp.bfloat16
        )
        run_partial_out = jnp.dot(activation, w_out, preferred_element_type=jnp.float32)
        summed = lax.psum_scatter(
            run_partial_out.reshape(received.shape[0], run_count, D).astype(jnp.bfloat16),
            "tensor",
            scatter_dimension=2,
            tiled=True,
        )
        returned = lax.all_to_all(summed, "expert", split_axis=0, concat_axis=0, tiled=True)
        returned_wide = returned.reshape(experts * capacity, own_width).astype(jnp.float32)
        mixture = jnp.dot(combine_table, returned_wide, precision=lax.Precision.HIGHEST)
        results.append((hidden_own.astype(jnp.float32) + mixture).astype(jnp.bfloat16))
    return jnp.stack(results)


def attend_steps(queries, new_kv, kv_cache, valid, sink_logits):
    row_count, kv_local = kv_cache.shape[0], kv_cache.shape[2]
    group_size = queries.shape[2] // (HD * kv_local)
    fresh = new_kv.reshape(STEPS, row_count, 2, kv_local, HD).transpose(2, 1, 3, 0, 4)
    key_all = jnp.concatenate([kv_cache[:, 0], fresh[0]], axis=2)
    value_all = jnp.concatenate([kv_cache[:, 1], fresh[1]], axis=2)
    asked = queries.reshape(STEPS, row_count, kv_local, group_size, HD)
    asked = asked.transpose(1, 2, 0, 3, 4).reshape(row_count, kv_local, STEPS * group_size, HD)
    step_of = jnp.arange(STEPS * group_size, dtype=jnp.int32) // group_size
    seen_new = jnp.arange(STEPS, dtype=jnp.int32)[None, :] <= step_of[:, None]
    seen = jnp.concatenate(
        [
            jnp.broadcast_to(valid[:, None, :], (row_count, STEPS * group_size, CACHE)),
            jnp.broadcast_to(seen_new[None], (row_count, STEPS * group_size, STEPS)),
        ],
        axis=2,
    )[:, None]
    scores = jnp.einsum("rkgd,rkjd->rkgj", asked, key_all, preferred_element_type=jnp.float32)
    scores = jnp.where(seen, scores * HD ** (-0.5), -jnp.inf)
    sinks = jnp.tile(sink_logits.reshape(kv_local, group_size), (1, STEPS))[None, :, :, None]
    peak = jnp.maximum(jnp.max(scores, axis=3, keepdims=True), sinks)
    weights = jnp.exp(scores - peak)
    totals = jnp.sum(weights, axis=3, keepdims=True) + jnp.exp(sinks - peak)
    probs = (weights / totals).astype(jnp.bfloat16)
    mixed = jnp.einsum("rkgj,rkjd->rkgd", probs, value_all, preferred_element_type=jnp.float32)
    mixed = mixed.astype(jnp.bfloat16).reshape(row_count, kv_local, STEPS, group_size, HD)
    return mixed.transpose(2, 0, 1, 3, 4).reshape(STEPS * row_count, -1)


WIDE = 3072
HALF = WIDE // 2
LANES = 128
SHARE_AT = WIDE - LANES
PAIRS = 192


def expert_kernel(
    zs,
    experts,
    projected_ref,
    residual_ref,
    gain_ref,
    pieces_ref,
    w_in_hbm,
    w_down_hbm,
    out_ref,
    w_in,
    w_down,
    w_gate,
    w_up,
    slots,
    act,
    kept,
    sib_out,
    sib_in,
    x_out,
    x_in,
    z_out,
    z_in,
    load_sem,
    own_send,
    own_recv,
    pass_send,
    core_send,
    core_recv,
    sib_send,
    sib_recv,
    xs_send,
    xs_recv,
    zs_send,
    zs_recv,
    sum_out,
    sum_in,
    hidden_own,
    sum_sem,
):
    group, me, core = lax.axis_index("groups"), lax.axis_index("expert"), lax.axis_index("tensor")
    z, x = me // 2, me % 2
    own_width = out_ref.shape[1]
    both = projected_ref.shape[0]
    width = 2 * own_width
    hidden_local = w_gate.shape[1]

    def device(to_z, to_x, to_core):
        return (group, to_z * 2 + to_x, to_core)

    peers = [device(lax.rem(z + d, zs), x, core) for d in range(1, zs)]
    other_x = device(z, 1 - x, core)
    other_core = device(z, x, 1 - core)
    barrier = pltpu.get_barrier_semaphore()
    for peer in peers + [other_x, other_core]:
        pl.semaphore_signal(barrier, inc=1, device_id=peer, device_id_type=pl.DeviceIdType.MESH)
    load_in = pltpu.make_async_copy(w_in_hbm, w_in, load_sem.at[0])
    load_in.start()
    load_down = pltpu.make_async_copy(w_down_hbm, w_down.at[pl.ds(0, width)], load_sem.at[1])
    load_down.start()
    w_down[width:, :] = jnp.zeros((w_down.shape[0] - width, hidden_local), jnp.bfloat16)
    mine = x * zs + z

    @pl.when(core == 0)
    def _():
        sum_out[:, :own_width] = projected_ref[:, :own_width] + residual_ref[...].astype(
            jnp.float32
        )
        sum_out[:, own_width:] = projected_ref[:, own_width:]

    @pl.when(core == 1)
    def _():
        sum_out[:, :own_width] = projected_ref[:, :own_width]
        sum_out[:, own_width:] = projected_ref[:, own_width:] + residual_ref[...].astype(
            jnp.float32
        )

    pl.semaphore_wait(barrier, zs + 1)

    def remote(src, dst, send, recv, to):
        return pltpu.make_async_remote_copy(
            src_ref=src,
            dst_ref=dst,
            send_sem=send,
            recv_sem=recv,
            device_id=to,
            device_id_type=pl.DeviceIdType.MESH,
        )

    def part(slot, half):
        return slots.at[slot, :, pl.ds(pl.multiple_of(half * HALF, HALF), HALF)]

    started = []
    exchange = remote(sum_out, sum_in, sum_sem.at[0], sum_sem.at[1], other_core)
    exchange.start()
    started.append(exchange)
    slots[mine, :, SHARE_AT - LANES :] = jnp.zeros((both, 2 * LANES), jnp.bfloat16)
    slots[mine, :, SHARE_AT:] = pieces_ref[...]
    exchange.wait_recv()
    hidden = (sum_out[...] + sum_in[...]).astype(jnp.bfloat16)

    @pl.when(core == 0)
    def _():
        hidden_own[...] = hidden[:, :own_width]

    @pl.when(core == 1)
    def _():
        hidden_own[...] = hidden[:, own_width:]

    widened = hidden.astype(jnp.float32)
    inv_rms = lax.rsqrt(jnp.mean(widened * widened, axis=1, keepdims=True) + 1e-05)
    normed = widened * inv_rms * gain_ref[...].astype(jnp.float32)
    slots[mine, :, :width] = normed.astype(jnp.bfloat16)

    def spread(slot, send, recv, to):
        copy = remote(part(slot, core), part(slot, core), send, recv.at[slot], to)
        copy.start()
        started.append(copy)

    def arrived(slot, half, recv):
        remote(part(slot, half), part(slot, half), own_send.at[0], recv.at[slot], other_x).wait_recv()

    spread(mine, own_send.at[0], own_recv, other_x)
    for d in range(1, zs):
        spread(mine, own_send.at[d], own_recv, peers[d - 1])

    row = lax.broadcasted_iota(jnp.int32, (PAIRS, 2 * PAIRS), 0)
    column = lax.broadcasted_iota(jnp.int32, (PAIRS, 2 * PAIRS), 1)
    evens = jnp.where(column == 2 * row, 1.0, 0.0).astype(jnp.bfloat16)
    odds = jnp.where(column == 2 * row + 1, 1.0, 0.0).astype(jnp.bfloat16)

    def separate(start, stop):
        def one(i, carry):
            at = pl.ds(pl.multiple_of(i * PAIRS, PAIRS), PAIRS)
            block = w_in[at, :, :].reshape(2 * PAIRS, hidden_local)
            w_gate[at, :] = jnp.dot(evens, block, preferred_element_type=jnp.float32).astype(
                jnp.bfloat16
            )
            w_up[at, :] = jnp.dot(odds, block, preferred_element_type=jnp.float32).astype(
                jnp.bfloat16
            )
            return carry

        lax.fori_loop(start, stop, one, 0)

    blocks = width // PAIRS
    load_in.wait()
    for d in range(1, zs):
        separate(blocks * (d - 1) // (zs - 1), blocks * d // (zs - 1))
        slot = x * zs + lax.rem(z + zs - d, zs)
        arrived(slot, core, own_recv)
        spread(slot, pass_send.at[d], own_recv, other_x)
        spread(slot, core_send.at[d], core_recv, other_core)
    load_down.wait()

    def first(side, at_x):
        def one(c, carry):
            at = pl.ds(pl.multiple_of(c * 256, 256), 256)
            inputs = slots[pl.ds(at_x * zs, zs), :, :width].reshape(zs * both, width)
            gate = jnp.dot(inputs, w_gate[:, at], preferred_element_type=jnp.float32)
            up = jnp.dot(inputs, w_up[:, at], preferred_element_type=jnp.float32)
            value = gate * jax.nn.sigmoid(1.702 * gate) * (up + 1.0)
            act[side, :, at] = value.astype(jnp.bfloat16)
            return carry

        lax.fori_loop(0, hidden_local // 256, one, 0)

    for d in range(1, zs):
        arrived(x * zs + lax.rem(z + zs - d, zs), 1 - core, core_recv)
    first(0, x)
    for d in range(zs):
        slot = (1 - x) * zs + lax.rem(z + zs - d, zs)
        arrived(slot, core, own_recv)
        spread(slot, core_send.at[zs + d], core_recv, other_core)
    for d in range(zs):
        arrived((1 - x) * zs + lax.rem(z + zs - d, zs), 1 - core, core_recv)
    first(1, 1 - x)

    def second(side, at_x):
        lane = lax.broadcasted_iota(jnp.int32, (1, LANES), 1)
        taken = (lax.rem(lane, experts) == me) & (lane < 3 * experts)
        shares = slots[pl.ds(at_x * zs, zs), :, SHARE_AT:].reshape(zs * both, LANES)
        share = jnp.sum(jnp.where(taken, shares.astype(jnp.float32), 0.0), axis=1, keepdims=True)

        def outputs(half, c):
            start = pl.multiple_of(half * own_width + c * 512, 16)
            return lax.dot_general(
                act[side],
                w_down[pl.ds(start, 512), :],
                (((1,), (1,)), ((), ())),
                preferred_element_type=jnp.float32,
            )

        def tile(c, carry):
            at = pl.ds(pl.multiple_of(c * 512, 512), 512)
            given = (outputs(1 - core, c) * share).astype(jnp.bfloat16)
            sib_out[side, :, :, at] = given.reshape(zs, both, 512)
            return carry

        def own_tile(c, carry):
            at = pl.ds(pl.multiple_of(c * 512, 512), 512)
            kept[side, :, :, at] = (outputs(core, c) * share).reshape(zs, both, 512)
            return carry

        lax.fori_loop(0, HALF // 512, tile, 0)
        copy = remote(
            sib_out.at[side], sib_in.at[side], sib_send.at[side], sib_recv.at[side], other_core
        )
        copy.start()
        lax.fori_loop(0, HALF // 512, own_tile, 0)
        return copy

    across = second(1, 1 - x)
    across.wait_recv()
    started.append(across)
    x_copies = []
    for d in range(zs):
        to_z = lax.rem(z + d + 1, zs)
        x_out[d] = (kept[1, to_z] + sib_in[1, to_z].astype(jnp.float32)).astype(jnp.bfloat16)
        copy = remote(x_out.at[d], x_in.at[d], xs_send.at[d], xs_recv.at[d], other_x)
        copy.start()
        x_copies.append(copy)
        started.append(copy)
    along = second(0, x)
    along.wait_recv()
    started.append(along)
    z_copies = []
    for d in range(zs):
        to_z = lax.rem(z + d + 1, zs)
        x_copies[d].wait_recv()
        total = kept[0, to_z] + sib_in[0, to_z].astype(jnp.float32) + x_in[d].astype(jnp.float32)
        if d < zs - 1:
            z_out[d] = total.astype(jnp.bfloat16)
            copy = remote(z_out.at[d], z_in.at[d], zs_send.at[d], zs_recv.at[d], peers[d])
            copy.start()
            z_copies.append(copy)
            started.append(copy)
    for d in range(zs - 1):
        z_copies[d].wait_recv()
        total = total + z_in[d].astype(jnp.float32)
    out_ref[...] = (hidden_own[...].astype(jnp.float32) + total[:, :own_width]).astype(
        out_ref.dtype
    )
    for copy in started:
        copy.wait_send()


def run_experts(projected, residual, gain, pieces, w_in, w_down, experts):
    both, own_width = residual.shape
    zs = experts // 2
    width, hidden_local = w_down.shape
    bf16, dma = jnp.bfloat16, pltpu.SemaphoreType.DMA
    vmem = pl.BlockSpec(memory_space=pltpu.VMEM)
    anywhere = pl.BlockSpec(memory_space=pl.ANY)
    return pl.pallas_call(
        functools.partial(expert_kernel, zs, experts),
        out_shape=jax.ShapeDtypeStruct((both, own_width), bf16),
        in_specs=[vmem, vmem, vmem, vmem, anywhere, anywhere],
        out_specs=vmem,
        scratch_shapes=[
            pltpu.VMEM(w_in.shape, bf16),
            pltpu.VMEM((own_width + HALF, hidden_local), bf16),
            pltpu.VMEM((width, hidden_local), bf16),
            pltpu.VMEM((width, hidden_local), bf16),
            pltpu.VMEM((experts, both, WIDE), bf16),
            pltpu.VMEM((2, zs * both, hidden_local), bf16),
            pltpu.VMEM((2, zs, both, HALF), jnp.float32),
            pltpu.VMEM((2, zs, both, HALF), bf16),
            pltpu.VMEM((2, zs, both, HALF), bf16),
            pltpu.VMEM((zs, both, HALF), bf16),
            pltpu.VMEM((zs, both, HALF), bf16),
            pltpu.VMEM((zs - 1, both, HALF), bf16),
            pltpu.VMEM((zs - 1, both, HALF), bf16),
            dma((2,)),
            dma((zs,)),
            dma((experts,)),
            dma((zs,)),
            dma((experts,)),
            dma((experts,)),
            dma((2,)),
            dma((2,)),
            dma((zs,)),
            dma((zs,)),
            dma((zs - 1,)),
            dma((zs - 1,)),
            pltpu.VMEM((both, width), jnp.float32),
            pltpu.VMEM((both, width), jnp.float32),
            pltpu.VMEM((both, own_width), bf16),
            dma((2,)),
        ],
        compiler_params=pltpu.CompilerParams(
            collective_id=0, has_side_effects=True, vmem_limit_bytes=56 * 2**20
        ),
        cost_estimate=pl.CostEstimate(
            flops=6 * experts * both * width * hidden_local,
            bytes_accessed=14 * 2**20,
            transcendentals=0,
        ),
    )(projected, residual, gain, pieces, w_in, w_down)


def body_dense(
    residual,
    queries,
    new_kv,
    kv_cache,
    lengths,
    sink_logits,
    out_proj,
    norm_gain,
    expert_ids,
    gate_weights,
    w_gate_up,
    w_down,
):
    row_count, own_width = residual.shape[1:]
    experts = lax.axis_size("expert")
    both = STEPS * row_count
    valid = jnp.arange(CACHE, dtype=jnp.int32)[None, :] < lengths[:, None]
    heads = attend_steps(queries, new_kv, kv_cache, valid, sink_logits)
    projected = jnp.dot(heads, out_proj, preferred_element_type=jnp.float32)
    named = expert_ids[..., None] == jnp.arange(experts, dtype=jnp.int32)
    share = jnp.sum(jnp.where(named, gate_weights[..., None], 0.0), axis=2).reshape(both, experts)
    pieces = []
    for unused in range(3):
        piece = lax.reduce_precision(share, 8, 7)
        pieces.append(piece.astype(jnp.bfloat16))
        share = share - piece
    pieces = jnp.concatenate(pieces, axis=1)
    pieces = jnp.pad(pieces, ((0, 0), (0, LANES - pieces.shape[1])))
    out = run_experts(
        projected,
        residual.reshape(both, own_width),
        norm_gain[None],
        pieces,
        w_gate_up[0],
        w_down[0].T,
        experts,
    )
    return out.reshape(STEPS, row_count, own_width)


def body(residual, *rest):
    row_count, experts = residual.shape[1], lax.axis_size("expert")
    compact = 2 * row_count * TOP // experts < row_count
    return (body_compact if compact else body_dense)(residual, *rest)


def solution(mesh):
    in_specs = (
        P(None, ("groups", "expert"), "tensor"),
        P(None, ("groups", "expert"), "tensor"),
        P(None, ("groups", "expert"), None, "tensor"),
        P(("groups", "expert"), None, "tensor", None, None),
        P(("groups", "expert")),
        P("tensor"),
        P("tensor", None),
        P(),
        P(None, ("groups", "expert"), None),
        P(None, ("groups", "expert"), None),
        P("expert", None, None, "tensor"),
        P("expert", "tensor", None),
    )
    out_specs = P(None, ("groups", "expert"), "tensor")
    return jax.shard_map(body, mesh=mesh, in_specs=in_specs, out_specs=out_specs, check_vma=False)
```

```python
import functools
import jax
import jax.numpy as jnp
from jax import lax
from jax.experimental import pallas as pl
from jax.experimental.pallas import tpu as pltpu
from jax.sharding import PartitionSpec as P

D = 2880
HD = 64
TOP = 4
STEPS = 2
CACHE = 32


def routing_tables(expert_now, weight_now, experts, capacity):
    row_count, top_count = expert_now.shape
    flattened = expert_now.reshape(-1)
    onehot = (flattened[:, None] == jnp.arange(experts, dtype=jnp.int32)[None, :]).astype(jnp.int32)
    earlier = jnp.cumsum(onehot, axis=0) - onehot
    slot_index = flattened * capacity + jnp.sum(earlier * onehot, axis=1)
    matches = slot_index[None, :] == jnp.arange(experts * capacity, dtype=jnp.int32)[:, None]
    matches = matches.reshape(experts * capacity, row_count, top_count)
    scatter_table = jnp.sum(matches.astype(jnp.int32), axis=2).astype(jnp.bfloat16)
    combine_table = jnp.sum(jnp.where(matches, weight_now[None, :, :], 0.0), axis=2).T
    return (scatter_table, combine_table)


def attend_local(queries_now, key_cache, value_cache, fresh_keys, fresh_values, valid, sink_logits):
    factor = HD ** (-0.5)
    cached = (
        jnp.einsum("rkgd,rkjd->rkgj", queries_now, key_cache, preferred_element_type=jnp.float32)
        * factor
    )
    recent = (
        jnp.einsum("rkgd,rkjd->rkgj", queries_now, fresh_keys, preferred_element_type=jnp.float32)
        * factor
    )
    cached = jnp.where(valid[:, None, None, :], cached, -jnp.inf)
    sinks = sink_logits.reshape(1, queries_now.shape[1], queries_now.shape[2], 1)
    peak = jnp.maximum(
        jnp.maximum(jnp.max(cached, axis=3, keepdims=True), jnp.max(recent, axis=3, keepdims=True)),
        sinks,
    )
    cached_weights = jnp.where(valid[:, None, None, :], jnp.exp(cached - peak), 0.0)
    recent_weights = jnp.exp(recent - peak)
    totals = (
        jnp.sum(cached_weights, axis=3, keepdims=True)
        + jnp.sum(recent_weights, axis=3, keepdims=True)
        + jnp.exp(sinks - peak)
    )
    cached_probs = (cached_weights / totals).astype(jnp.bfloat16)
    recent_probs = (recent_weights / totals).astype(jnp.bfloat16)
    mixed = jnp.einsum(
        "rkgj,rkjd->rkgd", cached_probs, value_cache, preferred_element_type=jnp.float32
    )
    mixed = mixed + jnp.einsum(
        "rkgj,rkjd->rkgd", recent_probs, fresh_values, preferred_element_type=jnp.float32
    )
    return mixed.astype(jnp.bfloat16).reshape(queries_now.shape[0], -1)


def body_compact(
    residual,
    queries,
    new_kv,
    kv_cache,
    lengths,
    sink_logits,
    out_proj,
    norm_gain,
    expert_ids,
    gate_weights,
    w_gate_up,
    w_down,
):
    row_count = residual.shape[1]
    own_width = residual.shape[2]
    experts = lax.axis_size("expert")
    tensor_rank = lax.axis_index("tensor")
    capacity = min(row_count, 2 * row_count * TOP // experts)
    kv_local = kv_cache.shape[2]
    group_size = queries.shape[2] // (HD * kv_local)
    hidden_local = w_down.shape[1]
    w_in = w_gate_up.reshape(D, 2 * hidden_local)
    w_out = w_down.reshape(hidden_local, D)
    col_start = tensor_rank * own_width
    gain_wide = norm_gain.astype(jnp.float32)
    valid = jnp.arange(CACHE, dtype=jnp.int32)[None, :] < lengths[:, None]
    results = []
    for step_index in range(STEPS):
        count = step_index + 1
        fresh = new_kv[:count].reshape(count, row_count, 2, kv_local, HD).transpose(2, 1, 3, 0, 4)
        queries_now = queries[step_index].reshape(row_count, kv_local, group_size, HD)
        heads = attend_local(
            queries_now, kv_cache[:, 0], kv_cache[:, 1], fresh[0], fresh[1], valid, sink_logits
        )
        projected = jnp.dot(heads, out_proj, preferred_element_type=jnp.float32)
        own_cols = lax.dynamic_slice_in_dim(projected, col_start, own_width, 1) + residual[
            step_index
        ].astype(jnp.float32)
        with_input = lax.dynamic_update_slice_in_dim(projected, own_cols, col_start, 1)
        scatter_table, combine_table = routing_tables(
            expert_ids[step_index], gate_weights[step_index], experts, capacity
        )
        hidden_full = lax.psum(with_input, "tensor").astype(jnp.bfloat16)
        widened = lax.optimization_barrier(hidden_full).astype(jnp.float32)
        inv_rms = lax.rsqrt(jnp.mean(widened * widened, axis=1, keepdims=True) + 1e-05)
        normed = (widened * inv_rms * gain_wide).astype(jnp.bfloat16)
        hidden_own = lax.dynamic_slice_in_dim(hidden_full, col_start, own_width, 1)
        outgoing = jnp.dot(scatter_table, normed, preferred_element_type=jnp.float32).astype(
            jnp.bfloat16
        )
        outgoing = outgoing.reshape(experts, capacity, D)
        received = lax.all_to_all(outgoing, "expert", split_axis=0, concat_axis=0, tiled=True)
        run_count = received.shape[1]
        gate_up = jnp.dot(
            received.reshape(-1, D), w_in, preferred_element_type=jnp.float32
        ).reshape(-1, 2, hidden_local)
        gate_part = gate_up[:, 0, :]
        up_part = gate_up[:, 1, :]
        activation = (gate_part * jax.nn.sigmoid(1.702 * gate_part) * (up_part + 1.0)).astype(
            jnp.bfloat16
        )
        run_partial_out = jnp.dot(activation, w_out, preferred_element_type=jnp.float32)
        summed = lax.psum_scatter(
            run_partial_out.reshape(received.shape[0], run_count, D).astype(jnp.bfloat16),
            "tensor",
            scatter_dimension=2,
            tiled=True,
        )
        returned = lax.all_to_all(summed, "expert", split_axis=0, concat_axis=0, tiled=True)
        returned_wide = returned.reshape(experts * capacity, own_width).astype(jnp.float32)
        mixture = jnp.dot(combine_table, returned_wide, precision=lax.Precision.HIGHEST)
        results.append((hidden_own.astype(jnp.float32) + mixture).astype(jnp.bfloat16))
    return jnp.stack(results)


def attend_steps(queries, new_kv, kv_cache, valid, sink_logits):
    row_count, kv_local = kv_cache.shape[0], kv_cache.shape[2]
    group_size = queries.shape[2] // (HD * kv_local)
    fresh = new_kv.reshape(STEPS, row_count, 2, kv_local, HD).transpose(2, 1, 3, 0, 4)
    key_all = jnp.concatenate([kv_cache[:, 0], fresh[0]], axis=2)
    value_all = jnp.concatenate([kv_cache[:, 1], fresh[1]], axis=2)
    asked = queries.reshape(STEPS, row_count, kv_local, group_size, HD)
    asked = asked.transpose(1, 2, 0, 3, 4).reshape(row_count, kv_local, STEPS * group_size, HD)
    step_of = jnp.arange(STEPS * group_size, dtype=jnp.int32) // group_size
    seen_new = jnp.arange(STEPS, dtype=jnp.int32)[None, :] <= step_of[:, None]
    seen = jnp.concatenate(
        [
            jnp.broadcast_to(valid[:, None, :], (row_count, STEPS * group_size, CACHE)),
            jnp.broadcast_to(seen_new[None], (row_count, STEPS * group_size, STEPS)),
        ],
        axis=2,
    )[:, None]
    scores = jnp.einsum("rkgd,rkjd->rkgj", asked, key_all, preferred_element_type=jnp.float32)
    scores = jnp.where(seen, scores * HD ** (-0.5), -jnp.inf)
    sinks = jnp.tile(sink_logits.reshape(kv_local, group_size), (1, STEPS))[None, :, :, None]
    peak = jnp.maximum(jnp.max(scores, axis=3, keepdims=True), sinks)
    weights = jnp.exp(scores - peak)
    totals = jnp.sum(weights, axis=3, keepdims=True) + jnp.exp(sinks - peak)
    probs = (weights / totals).astype(jnp.bfloat16)
    mixed = jnp.einsum("rkgj,rkjd->rkgd", probs, value_all, preferred_element_type=jnp.float32)
    mixed = mixed.astype(jnp.bfloat16).reshape(row_count, kv_local, STEPS, group_size, HD)
    return mixed.transpose(2, 0, 1, 3, 4).reshape(STEPS * row_count, -1)


WIDE = 3072
HALF = WIDE // 2
LANES = 128
SHARE_AT = WIDE - LANES
PAIRS = 192


def expert_kernel(
    zs,
    experts,
    projected_ref,
    residual_ref,
    gain_ref,
    pieces_ref,
    w_in_hbm,
    w_down_hbm,
    out_ref,
    w_in,
    w_down,
    w_gate,
    w_up,
    slots,
    act,
    kept,
    sib_out,
    sib_in,
    x_out,
    x_in,
    z_out,
    z_in,
    load_sem,
    own_send,
    own_recv,
    pass_send,
    core_send,
    core_recv,
    sib_send,
    sib_recv,
    xs_send,
    xs_recv,
    zs_send,
    zs_recv,
    sum_out,
    sum_in,
    hidden_own,
    sum_sem,
):
    group, me, core = lax.axis_index("groups"), lax.axis_index("expert"), lax.axis_index("tensor")
    z, x = me // 2, me % 2
    own_width = out_ref.shape[1]
    both = projected_ref.shape[0]
    width = 2 * own_width
    hidden_local = w_gate.shape[1]

    def device(to_z, to_x, to_core):
        return (group, to_z * 2 + to_x, to_core)

    peers = [device(lax.rem(z + d, zs), x, core) for d in range(1, zs)]
    other_x = device(z, 1 - x, core)
    other_core = device(z, x, 1 - core)
    barrier = pltpu.get_barrier_semaphore()
    for peer in peers + [other_x, other_core]:
        pl.semaphore_signal(barrier, inc=1, device_id=peer, device_id_type=pl.DeviceIdType.MESH)
    load_in = pltpu.make_async_copy(w_in_hbm, w_in, load_sem.at[0])
    load_in.start()
    load_down = pltpu.make_async_copy(w_down_hbm, w_down.at[pl.ds(0, width)], load_sem.at[1])
    load_down.start()
    w_down[width:, :] = jnp.zeros((w_down.shape[0] - width, hidden_local), jnp.bfloat16)
    mine = x * zs + z

    @pl.when(core == 0)
    def _():
        sum_out[:, :own_width] = projected_ref[:, :own_width] + residual_ref[...].astype(
            jnp.float32
        )
        sum_out[:, own_width:] = projected_ref[:, own_width:]

    @pl.when(core == 1)
    def _():
        sum_out[:, :own_width] = projected_ref[:, :own_width]
        sum_out[:, own_width:] = projected_ref[:, own_width:] + residual_ref[...].astype(
            jnp.float32
        )

    pl.semaphore_wait(barrier, zs + 1)

    def remote(src, dst, send, recv, to):
        return pltpu.make_async_remote_copy(
            src_ref=src,
            dst_ref=dst,
            send_sem=send,
            recv_sem=recv,
            device_id=to,
            device_id_type=pl.DeviceIdType.MESH,
        )

    def part(slot, half):
        return slots.at[slot, :, pl.ds(pl.multiple_of(half * HALF, HALF), HALF)]

    started = []
    exchange = remote(sum_out, sum_in, sum_sem.at[0], sum_sem.at[1], other_core)
    exchange.start()
    started.append(exchange)
    slots[mine, :, SHARE_AT - LANES :] = jnp.zeros((both, 2 * LANES), jnp.bfloat16)
    slots[mine, :, SHARE_AT:] = pieces_ref[...]
    exchange.wait_recv()
    hidden = (sum_out[...] + sum_in[...]).astype(jnp.bfloat16)

    @pl.when(core == 0)
    def _():
        hidden_own[...] = hidden[:, :own_width]

    @pl.when(core == 1)
    def _():
        hidden_own[...] = hidden[:, own_width:]

    widened = hidden.astype(jnp.float32)
    inv_rms = lax.rsqrt(jnp.mean(widened * widened, axis=1, keepdims=True) + 1e-05)
    normed = widened * inv_rms * gain_ref[...].astype(jnp.float32)
    slots[mine, :, :width] = normed.astype(jnp.bfloat16)

    def spread(slot, send, recv, to):
        copy = remote(part(slot, core), part(slot, core), send, recv.at[slot], to)
        copy.start()
        started.append(copy)

    def arrived(slot, half, recv):
        remote(part(slot, half), part(slot, half), own_send.at[0], recv.at[slot], other_x).wait_recv()

    spread(mine, own_send.at[0], own_recv, other_x)
    for d in range(1, zs):
        spread(mine, own_send.at[d], own_recv, peers[d - 1])

    row = lax.broadcasted_iota(jnp.int32, (PAIRS, 2 * PAIRS), 0)
    column = lax.broadcasted_iota(jnp.int32, (PAIRS, 2 * PAIRS), 1)
    evens = jnp.where(column == 2 * row, 1.0, 0.0).astype(jnp.bfloat16)
    odds = jnp.where(column == 2 * row + 1, 1.0, 0.0).astype(jnp.bfloat16)

    def separate(start, stop):
        def one(i, carry):
            at = pl.ds(pl.multiple_of(i * PAIRS, PAIRS), PAIRS)
            block = w_in[at, :, :].reshape(2 * PAIRS, hidden_local)
            w_gate[at, :] = jnp.dot(evens, block, preferred_element_type=jnp.float32).astype(
                jnp.bfloat16
            )
            w_up[at, :] = jnp.dot(odds, block, preferred_element_type=jnp.float32).astype(
                jnp.bfloat16
            )
            return carry

        lax.fori_loop(start, stop, one, 0)

    blocks = width // PAIRS
    load_in.wait()
    for d in range(1, zs):
        separate(blocks * (d - 1) // (zs - 1), blocks * d // (zs - 1))
        slot = x * zs + lax.rem(z + zs - d, zs)
        arrived(slot, core, own_recv)
        spread(slot, pass_send.at[d], own_recv, other_x)
        spread(slot, core_send.at[d], core_recv, other_core)
    load_down.wait()

    def first(side, at_x):
        def one(c, carry):
            at = pl.ds(pl.multiple_of(c * 256, 256), 256)
            inputs = slots[pl.ds(at_x * zs, zs), :, :width].reshape(zs * both, width)
            gate = jnp.dot(inputs, w_gate[:, at], preferred_element_type=jnp.float32)
            up = jnp.dot(inputs, w_up[:, at], preferred_element_type=jnp.float32)
            value = gate * jax.nn.sigmoid(1.702 * gate) * (up + 1.0)
            act[side, :, at] = value.astype(jnp.bfloat16)
            return carry

        lax.fori_loop(0, hidden_local // 256, one, 0)

    for d in range(1, zs):
        arrived(x * zs + lax.rem(z + zs - d, zs), 1 - core, core_recv)

    def relay(start, stop):
        for d in range(start, stop):
            slot = (1 - x) * zs + lax.rem(z + zs - d, zs)
            arrived(slot, core, own_recv)
            spread(slot, core_send.at[zs + d], core_recv, other_core)

    relay(0, zs // 2)
    first(0, x)
    relay(zs // 2, zs)
    for d in range(zs):
        arrived((1 - x) * zs + lax.rem(z + zs - d, zs), 1 - core, core_recv)
    first(1, 1 - x)

    def second(side, at_x):
        lane = lax.broadcasted_iota(jnp.int32, (1, LANES), 1)
        taken = (lax.rem(lane, experts) == me) & (lane < 3 * experts)
        shares = slots[pl.ds(at_x * zs, zs), :, SHARE_AT:].reshape(zs * both, LANES)
        share = jnp.sum(jnp.where(taken, shares.astype(jnp.float32), 0.0), axis=1, keepdims=True)

        def outputs(half, c):
            start = pl.multiple_of(half * own_width + c * 512, 16)
            return lax.dot_general(
                act[side],
                w_down[pl.ds(start, 512), :],
                (((1,), (1,)), ((), ())),
                preferred_element_type=jnp.float32,
            )

        def tile(c, carry):
            at = pl.ds(pl.multiple_of(c * 512, 512), 512)
            given = (outputs(1 - core, c) * share).astype(jnp.bfloat16)
            sib_out[side, :, :, at] = given.reshape(zs, both, 512)
            return carry

        def own_tile(c, carry):
            at = pl.ds(pl.multiple_of(c * 512, 512), 512)
            kept[side, :, :, at] = (outputs(core, c) * share).reshape(zs, both, 512)
            return carry

        lax.fori_loop(0, HALF // 512, tile, 0)
        copy = remote(
            sib_out.at[side], sib_in.at[side], sib_send.at[side], sib_recv.at[side], other_core
        )
        copy.start()
        lax.fori_loop(0, HALF // 512, own_tile, 0)
        return copy

    across = second(1, 1 - x)
    across.wait_recv()
    started.append(across)
    x_copies = []
    for d in range(zs):
        to_z = lax.rem(z + d + 1, zs)
        x_out[d] = (kept[1, to_z] + sib_in[1, to_z].astype(jnp.float32)).astype(jnp.bfloat16)
        copy = remote(x_out.at[d], x_in.at[d], xs_send.at[d], xs_recv.at[d], other_x)
        copy.start()
        x_copies.append(copy)
        started.append(copy)
    along = second(0, x)
    along.wait_recv()
    started.append(along)
    z_copies = []
    for d in range(zs):
        to_z = lax.rem(z + d + 1, zs)
        x_copies[d].wait_recv()
        total = kept[0, to_z] + sib_in[0, to_z].astype(jnp.float32) + x_in[d].astype(jnp.float32)
        if d < zs - 1:
            z_out[d] = total.astype(jnp.bfloat16)
            copy = remote(z_out.at[d], z_in.at[d], zs_send.at[d], zs_recv.at[d], peers[d])
            copy.start()
            z_copies.append(copy)
            started.append(copy)
    for d in range(zs - 1):
        z_copies[d].wait_recv()
        total = total + z_in[d].astype(jnp.float32)
    out_ref[...] = (hidden_own[...].astype(jnp.float32) + total[:, :own_width]).astype(
        out_ref.dtype
    )
    for copy in started:
        copy.wait_send()


def run_experts(projected, residual, gain, pieces, w_in, w_down, experts):
    both, own_width = residual.shape
    zs = experts // 2
    width, hidden_local = w_down.shape
    bf16, dma = jnp.bfloat16, pltpu.SemaphoreType.DMA
    vmem = pl.BlockSpec(memory_space=pltpu.VMEM)
    anywhere = pl.BlockSpec(memory_space=pl.ANY)
    return pl.pallas_call(
        functools.partial(expert_kernel, zs, experts),
        out_shape=jax.ShapeDtypeStruct((both, own_width), bf16),
        in_specs=[vmem, vmem, vmem, vmem, anywhere, anywhere],
        out_specs=vmem,
        scratch_shapes=[
            pltpu.VMEM(w_in.shape, bf16),
            pltpu.VMEM((own_width + HALF, hidden_local), bf16),
            pltpu.VMEM((width, hidden_local), bf16),
            pltpu.VMEM((width, hidden_local), bf16),
            pltpu.VMEM((experts, both, WIDE), bf16),
            pltpu.VMEM((2, zs * both, hidden_local), bf16),
            pltpu.VMEM((2, zs, both, HALF), jnp.float32),
            pltpu.VMEM((2, zs, both, HALF), bf16),
            pltpu.VMEM((2, zs, both, HALF), bf16),
            pltpu.VMEM((zs, both, HALF), bf16),
            pltpu.VMEM((zs, both, HALF), bf16),
            pltpu.VMEM((zs - 1, both, HALF), bf16),
            pltpu.VMEM((zs - 1, both, HALF), bf16),
            dma((2,)),
            dma((zs,)),
            dma((experts,)),
            dma((zs,)),
            dma((experts,)),
            dma((experts,)),
            dma((2,)),
            dma((2,)),
            dma((zs,)),
            dma((zs,)),
            dma((zs - 1,)),
            dma((zs - 1,)),
            pltpu.VMEM((both, width), jnp.float32),
            pltpu.VMEM((both, width), jnp.float32),
            pltpu.VMEM((both, own_width), bf16),
            dma((2,)),
        ],
        compiler_params=pltpu.CompilerParams(
            collective_id=0, has_side_effects=True, vmem_limit_bytes=56 * 2**20
        ),
        cost_estimate=pl.CostEstimate(
            flops=6 * experts * both * width * hidden_local,
            bytes_accessed=14 * 2**20,
            transcendentals=0,
        ),
    )(projected, residual, gain, pieces, w_in, w_down)


def body_dense(
    residual,
    queries,
    new_kv,
    kv_cache,
    lengths,
    sink_logits,
    out_proj,
    norm_gain,
    expert_ids,
    gate_weights,
    w_gate_up,
    w_down,
):
    row_count, own_width = residual.shape[1:]
    experts = lax.axis_size("expert")
    both = STEPS * row_count
    valid = jnp.arange(CACHE, dtype=jnp.int32)[None, :] < lengths[:, None]
    heads = attend_steps(queries, new_kv, kv_cache, valid, sink_logits)
    projected = jnp.dot(heads, out_proj, preferred_element_type=jnp.float32)
    named = expert_ids[..., None] == jnp.arange(experts, dtype=jnp.int32)
    share = jnp.sum(jnp.where(named, gate_weights[..., None], 0.0), axis=2).reshape(both, experts)
    pieces = []
    for unused in range(3):
        piece = lax.reduce_precision(share, 8, 7)
        pieces.append(piece.astype(jnp.bfloat16))
        share = share - piece
    pieces = jnp.concatenate(pieces, axis=1)
    pieces = jnp.pad(pieces, ((0, 0), (0, LANES - pieces.shape[1])))
    out = run_experts(
        projected,
        residual.reshape(both, own_width),
        norm_gain[None],
        pieces,
        w_gate_up[0],
        w_down[0].T,
        experts,
    )
    return out.reshape(STEPS, row_count, own_width)


def body(residual, *rest):
    row_count, experts = residual.shape[1], lax.axis_size("expert")
    compact = 2 * row_count * TOP // experts < row_count
    return (body_compact if compact else body_dense)(residual, *rest)


def solution(mesh):
    in_specs = (
        P(None, ("groups", "expert"), "tensor"),
        P(None, ("groups", "expert"), "tensor"),
        P(None, ("groups", "expert"), None, "tensor"),
        P(("groups", "expert"), None, "tensor", None, None),
        P(("groups", "expert")),
        P("tensor"),
        P("tensor", None),
        P(),
        P(None, ("groups", "expert"), None),
        P(None, ("groups", "expert"), None),
        P("expert", None, None, "tensor"),
        P("expert", "tensor", None),
    )
    out_specs = P(None, ("groups", "expert"), "tensor")
    return jax.shard_map(body, mesh=mesh, in_specs=in_specs, out_specs=out_specs, check_vma=False)
```
